32 devices in a mesh: group: 2 (over x), tok: 16 (over z, y, core).
Axes of the slice: x: 2, y: 2, z: 4, core: 2. Of those that a mesh axis runs over, the one named last changes fastest.
Arguments:
- hidden: bfloat16 [4096, 6144], P(('group', 'tok')), parts along dimension 0, may hold values from -6 to 6
- ln_gain: bfloat16 [6144], replicated, may hold values from 0.099609375 to 1.8984375
- router: bfloat16 [6144, 16], replicated, may hold values from -0.078125 to 0.078125
- routes: int32 [4096, 4], P(('group', 'tok')), parts along dimension 0, may hold values from 0 to 15, as said below
- w_gate: bfloat16 [16, 6144, 128], P('tok'), may hold values from -0.078125 to 0.078125
- w_up: bfloat16 [16, 6144, 128], P('tok'), may hold values from -0.078125 to 0.078125
- w_down: bfloat16 [16, 128, 6144], P('tok'), may hold values from -0.25 to 0.25
Outputs:
- mixed: bfloat16 [4096, 6144], P(('group', 'tok')), parts along dimension 0
The draws below stay inside these ranges and needn't reach their ends.
There are 2 independent parts, one for each index of `group`. The reference program is written for one: setup_inputs(seed, part) draws one part's arguments, and reference() takes and returns one part's arrays. A program takes and returns all parts, laid end to end along the dimension named above; an argument that names none is the same for every part. Nothing has to cross between parts.
Inputs may be any that keep to these rules, and one draw needn't show every extreme that they name: `routes`: the 4 experts of a row differ. In each aligned block of 64 rows (one micro-batch of one device) each served expert 0 to 1 is named by 1 to 4 rows, and one served expert, the same in all blocks of a part, by exactly 4; experts 2 and above have no such bound.
All inputs are finite; a program needn't handle non-finite values.
Results may differ from the reference program's by a relative error of at most 0.0026.
Values may be sent and summed in bfloat16 or wider, within the bound.
A program may use at most 128 MiB of HBM per device.

```python
import jax
import jax.numpy as jnp
from jax import lax

D = 6144
EXPERTS = 16
TOP = 4
EXP_WIN = 2
FF_DEV = 128
MB_ROWS = 64
MB_DEV = 2
MOST = 4
TOKENS = 2048
N_TOK = 16


def draw_routes(key, part):
    key = jax.random.fold_in(key, 11)
    blocks = TOKENS // MB_ROWS
    full_key, count_key, member_key, other_key = jax.random.split(key, 4)
    full_expert = jax.random.randint(full_key, (), 0, EXP_WIN)
    served_index = jnp.arange(EXP_WIN, dtype=jnp.int32)
    counts = jax.random.randint(count_key, (blocks, EXP_WIN), 1, MOST + 1)
    counts = jnp.where(served_index[None, :] == full_expert, MOST, counts)
    member_keys = jax.random.split(member_key, blocks * EXP_WIN)
    ranks = jax.vmap(lambda single: jax.random.permutation(single, MB_ROWS))(member_keys)
    ranks = ranks.reshape(blocks, EXP_WIN, MB_ROWS)
    member = (ranks < counts[:, :, None]).astype(jnp.int32)
    member = jnp.transpose(member, (0, 2, 1)).reshape(TOKENS, EXP_WIN)
    order = jnp.cumsum(member, axis=1) - 1
    served_count = jnp.sum(member, axis=1)
    slot_index = jnp.arange(TOP, dtype=jnp.int32)
    matches = (member[:, None, :] == 1) & (order[:, None, :] == slot_index[None, :, None])
    served_pick = jnp.sum(jnp.where(matches, served_index[None, None, :], 0), axis=2)
    other_keys = jax.random.split(other_key, TOKENS)
    others = jax.vmap(lambda single: jax.random.permutation(single, EXPERTS - EXP_WIN))(other_keys) + EXP_WIN
    shifted = jnp.clip(slot_index[None, :] - served_count[:, None], 0, EXPERTS - EXP_WIN - 1)
    other_pick = jnp.take_along_axis(others, shifted, axis=1)
    return jnp.where(slot_index[None, :] < served_count[:, None], served_pick, other_pick).astype(jnp.int32)


def steps_of(key, dims, pieces, smallest, high):
    level = 1.0
    for axis_at, shards_of in pieces:
        steps = jax.random.uniform(jax.random.fold_in(jax.random.fold_in(key, 6), axis_at), (shards_of,), jnp.float32, smallest / len(pieces), high / len(pieces))
        level = level * jnp.repeat(jnp.exp(steps), dims[axis_at] // shards_of).reshape((-1,) + (1,) * (len(dims) - 1 - axis_at))
    return level


def gaussian(own_key, dims, scale, limit, shards=(), kind=jnp.bfloat16):
    factor_of = steps_of(own_key, dims, shards, -0.22, 0.18) if shards else 1.0
    entries = jax.random.normal(own_key, dims, jnp.float32) * scale * factor_of
    return jnp.minimum(jnp.maximum(entries, -limit), limit).astype(kind)


def setup_inputs(seed: int = 0, part: int = 0) -> dict:
    arg_keys = jax.random.split(jax.random.key(seed), 8)
    part_keys = jax.random.split(jax.random.fold_in(arg_keys[7], part), 8)
    hidden = gaussian(part_keys[0], (TOKENS, D), 1.0, 6.0, ((0, 16),))
    ln_gain = jnp.clip(1.0 + 0.18 * jax.random.normal(arg_keys[1], (D,), jnp.float32), 0.099609375, 1.8984375).astype(jnp.bfloat16)
    router = gaussian(arg_keys[2], (D, EXPERTS), D ** -0.5, 0.078125)
    routes = draw_routes(jax.random.fold_in(jax.random.fold_in(arg_keys[7], part), 71), part)
    w_gate = gaussian(arg_keys[4], (N_TOK, D, FF_DEV), D ** -0.5, 0.078125, ((0, 16),))
    w_up = gaussian(arg_keys[5], (N_TOK, D, FF_DEV), D ** -0.5, 0.078125, ((0, 16),))
    w_down = gaussian(arg_keys[6], (N_TOK, FF_DEV, D), (FF_DEV * 4) ** -0.5, 0.25, ((0, 16),))
    return dict(hidden=hidden, ln_gain=ln_gain, router=router, routes=routes, w_gate=w_gate, w_up=w_up, w_down=w_down)


EPS = 1e-05

def layer_norm(hidden, ln_gain):
    values = hidden.astype(jnp.float32)
    center = lax.optimization_barrier(jnp.mean(values, axis=-1, keepdims=True))
    spread = lax.optimization_barrier(jnp.mean(jnp.square(values - center), axis=-1, keepdims=True))
    return ((values - center) * lax.rsqrt(spread + EPS) * ln_gain.astype(jnp.float32)).astype(jnp.bfloat16)

def gate_values(normed, router, routes):
    logits = jnp.dot(normed, router, preferred_element_type=jnp.float32)
    onehot = routes[:, :, None] == jnp.arange(EXPERTS, dtype=jnp.int32)[None, None, :]
    chosen = lax.optimization_barrier(jnp.sum(jnp.where(onehot, logits[:, None, :], jnp.zeros((), jnp.float32)), axis=-1))
    raised = jnp.exp(chosen)
    return (raised / lax.optimization_barrier(jnp.sum(raised, axis=-1, keepdims=True)), onehot)

def placement(onehot, routes, blocks, block_rows):
    pair_hot = onehot.reshape(blocks, block_rows * TOP, EXPERTS).astype(jnp.int32)
    earlier = jnp.cumsum(pair_hot, axis=1) - pair_hot
    placed = lax.optimization_barrier(jnp.sum(earlier * pair_hot, axis=-1)).astype(jnp.int32)
    expert_ids = routes.reshape(blocks, block_rows * TOP).astype(jnp.int32)
    return (expert_ids, placed)

def gather_rows(normed, slot_table):
    filled = slot_table >= 0
    picked = jnp.take(normed, jnp.maximum(slot_table, 0), axis=0)
    return jnp.where(filled[:, None], picked, jnp.zeros((), normed.dtype))

def expert_rows(send_rows, gate_mat, up_mat, down_mat):
    gate_out = jnp.dot(send_rows, gate_mat, preferred_element_type=jnp.float32)
    up_out = jnp.dot(send_rows, up_mat, preferred_element_type=jnp.float32)
    hidden_act = (jax.nn.silu(gate_out) * up_out).astype(jnp.bfloat16)
    return jnp.dot(hidden_act, down_mat, preferred_element_type=jnp.float32).astype(jnp.bfloat16)

def reference(hidden, ln_gain, router, routes, w_gate, w_up, w_down):
    windows = N_TOK // EXP_WIN
    blocks = TOKENS // MB_ROWS
    normed = layer_norm(hidden, ln_gain)
    gates, onehot = gate_values(normed, router, routes)
    expert_ids, placed = placement(onehot, routes, blocks, MB_ROWS)
    block_ids = jnp.arange(blocks, dtype=jnp.int32)[:, None]
    source = block_ids // MB_DEV
    micro_ids = block_ids % MB_DEV
    per_expert = N_TOK * MB_DEV * MOST
    slot = (source * MB_DEV + micro_ids) * MOST + placed
    served = expert_ids < EXP_WIN
    slot_flat = jnp.where(served, expert_ids * per_expert + slot, EXP_WIN * per_expert).reshape(-1).astype(jnp.int32)
    token_ids = (block_ids * MB_ROWS + jnp.arange(MB_ROWS * TOP, dtype=jnp.int32)[None, :] // TOP).reshape(-1)
    token_table = jnp.full((EXP_WIN * per_expert,), -1, jnp.int32).at[slot_flat].set(token_ids, mode='drop').reshape(EXP_WIN, per_expert)
    gate_table = jnp.zeros((EXP_WIN * per_expert,), jnp.float32).at[slot_flat].set(gates.reshape(-1), mode='drop').reshape(EXP_WIN, per_expert)

    def add_window(device_index, weighted):
        expert_index = device_index // windows
        slot_table = lax.dynamic_index_in_dim(token_table, expert_index, 0, keepdims=False)
        slot_gates = lax.dynamic_index_in_dim(gate_table, expert_index, 0, keepdims=False)
        send_rows = gather_rows(normed, slot_table)
        gate_mat = lax.dynamic_index_in_dim(w_gate, device_index, 0, keepdims=False)
        up_mat = lax.dynamic_index_in_dim(w_up, device_index, 0, keepdims=False)
        down_mat = lax.dynamic_index_in_dim(w_down, device_index, 0, keepdims=False)
        out_rows = expert_rows(send_rows, gate_mat, up_mat, down_mat)
        contrib = out_rows.astype(jnp.float32) * slot_gates[:, None]
        return weighted.at[jnp.maximum(slot_table, 0)].add(contrib)
    weighted = lax.fori_loop(0, N_TOK, add_window, jnp.zeros((TOKENS, D), jnp.float32))
    return (hidden.astype(jnp.float32) + weighted).astype(jnp.bfloat16)
```

```python
import functools

import jax
import jax.numpy as jnp
from jax import lax
from jax.experimental import pallas as pl
from jax.experimental.pallas import tpu as pltpu
from jax.sharding import PartitionSpec as P

EXPERTS = 16
TOP = 4
EXP_WIN = 2
MB_ROWS = 64
MB_DEV = 2
MOST = 4
SLOTS = MB_DEV * MOST

EPS = 1e-05
MESH = pl.DeviceIdType.MESH
F32 = jnp.float32
BF16 = jnp.bfloat16


def routes_plan(n):
    bits = n.bit_length() - 1
    inner = [1 << b for b in range(1, bits - 1)]
    half = n // 2
    orders = {0: inner[::-1], half: inner}

    def chain(slot):
        return half if slot & half else 0

    def later(slot):
        order = orders[chain(slot)]
        last = -1
        for at, bit in enumerate(order):
            if slot & bit:
                last = at
        return order[last + 1 :]

    def last_bit(slot):
        if slot & 1:
            return 1
        found = half
        for bit in orders[chain(slot)]:
            if slot & bit:
                found = bit
        return found

    evens = [slot for slot in range(n) if not slot & 1]

    def depth(slot):
        return bin(slot).count("1") + (1 if slot & half else 0)

    arrival = sorted([slot for slot in evens if slot], key=lambda slot: (depth(slot), slot & half))
    return later, last_bit, arrival


def kernel(n, hidden_hbm, gain_ref, router_hbm, routes_ref, wg_hbm, wu_hbm, wd_hbm, out_hbm,
           hidden, router, wg, wu, wd, x_buf, other, y_buf, z_buf, out,
           in_sem, out_sem, x_send, x_recv, z_send, z_recv):
    later, last_bit, arrival = routes_plan(n)
    half = n // 2
    tokens, width = hidden.shape
    cols = width // 2
    me = lax.axis_index("tok")

    def peer(bit):
        return {"tok": me + bit * (1 - 2 * lax.rem(lax.div(me, bit), 2))}

    load_hidden = pltpu.make_async_copy(hidden_hbm, hidden, in_sem.at[0])
    load_hidden.start()
    loads = [
        pltpu.make_async_copy(src, dst, in_sem.at[1 + at])
        for at, (src, dst) in enumerate(((router_hbm, router), (wg_hbm, wg), (wu_hbm, wu), (wd_hbm, wd)))
    ]
    for load in loads:
        load.start()

    barrier = pltpu.get_barrier_semaphore()
    bits = [1 << b for b in range(n.bit_length() - 1)]
    for bit in bits:
        pl.semaphore_signal(barrier, inc=1, device_id=peer(bit), device_id_type=MESH)

    my_expert = lax.div(me, half)
    token = lax.broadcasted_iota(jnp.int32, (2 * SLOTS, tokens), 1)
    slot_at = lax.broadcasted_iota(jnp.int32, (2 * SLOTS, tokens), 0)
    second = lax.div(slot_at, SLOTS)
    slot_expert = my_expert + second - 2 * my_expert * second
    routes = routes_ref[...]
    hits = jnp.zeros((2 * SLOTS, tokens), F32)
    for k in range(TOP):
        hits += jnp.where(routes[k : k + 1] == slot_expert, 1.0, 0.0)
    row = lax.broadcasted_iota(jnp.int32, (tokens, tokens), 0)
    lane = lax.broadcasted_iota(jnp.int32, (tokens, tokens), 1)
    earlier = (row < lane) & (lax.div(lane, MB_ROWS) == lax.div(row, MB_ROWS))
    rank = jnp.dot(hits.astype(BF16), jnp.where(earlier, 1.0, 0.0).astype(BF16), preferred_element_type=F32)
    slot_rank = lax.rem(slot_at, MOST)
    slot_block = lax.rem(lax.div(slot_at, MOST), MB_DEV)
    fits = (rank == slot_rank.astype(F32)) & (slot_block == lax.div(token, MB_ROWS))
    pick = jnp.where(fits, hits, 0.0)

    load_hidden.wait()
    rows = jnp.dot(pick.astype(BF16), hidden[...], preferred_element_type=F32)
    center = jnp.mean(rows, axis=-1, keepdims=True)
    rows = rows - center
    spread = jnp.mean(jnp.square(rows), axis=-1, keepdims=True)
    rows = rows * lax.rsqrt(spread + EPS) * gain_ref[...].astype(F32)

    def piece(values):
        return jnp.concatenate([values[:, :cols], values[:, cols:]], axis=0).astype(BF16)

    other[...] = piece(rows[SLOTS:])
    x_buf[0] = piece(rows[:SLOTS])

    pl.semaphore_wait(barrier, len(bits))

    def x_copy(src, slot, bit):
        return pltpu.make_async_remote_copy(
            src_ref=src, dst_ref=x_buf.at[slot], send_sem=x_send.at[slot], recv_sem=x_recv.at[slot],
            device_id=peer(bit), device_id_type=MESH)

    sent = [x_copy(other, half, half)]
    sent[-1].start()

    def pass_on(slot):
        for bit in later(slot):
            sent.append(x_copy(x_buf.at[slot], slot ^ bit, bit))
            sent[-1].start()
        sent.append(x_copy(x_buf.at[slot], slot ^ 1, 1))
        sent[-1].start()

    pass_on(0)

    normed = rows.astype(BF16)
    loads[0].wait()
    across = (((1,), (1,)), ((), ()))
    logits = lax.dot_general(normed, router[...], across, preferred_element_type=F32)
    expert_row = lax.broadcasted_iota(jnp.int32, (EXPERTS, tokens), 0)
    chosen = jnp.zeros((EXPERTS, tokens), F32)
    for k in range(TOP):
        chosen += jnp.where(routes[k : k + 1] == expert_row, 1.0, 0.0)
    slot_chosen = lax.dot_general(pick.astype(BF16), chosen.astype(BF16), across, preferred_element_type=F32)
    raised = jnp.where(slot_chosen > 0.5, jnp.exp(logits), 0.0)
    expert_lane = lax.broadcasted_iota(jnp.int32, (2 * SLOTS, EXPERTS), 1)
    top = jnp.sum(jnp.where(expert_lane == slot_expert[:, :EXPERTS], raised, 0.0), axis=-1, keepdims=True)
    total = jnp.sum(raised, axis=-1, keepdims=True)
    filled = jnp.sum(slot_chosen, axis=-1, keepdims=True) > 0.5
    gates = jnp.where(filled, top / jnp.where(filled, total, 1.0), 0.0)
    weighted = jnp.concatenate([pick * gates, jnp.zeros((128 - 2 * SLOTS, tokens), F32)], axis=0).T
    weighted = weighted[:, : 2 * SLOTS]

    for slot in arrival:
        x_copy(other, slot, last_bit(slot)).wait_recv()
        pass_on(slot)
    for slot in range(1, n, 2):
        x_copy(other, slot, 1).wait_recv()

    loads[1].wait()
    loads[2].wait()
    loads[3].wait()

    group = min(n, 16)

    def project(at, carry):
        base = pl.multiple_of(at * group, group)
        x = x_buf[pl.ds(base, group)].reshape(group * 2 * SLOTS, cols)
        w_lo = jnp.concatenate([wg[:cols], wu[:cols]], axis=1)
        w_hi = jnp.concatenate([wg[cols:], wu[cols:]], axis=1)
        lo = jnp.dot(x, w_lo, preferred_element_type=F32).reshape(group, 2 * SLOTS, -1)[:, :SLOTS]
        hi = jnp.dot(x, w_hi, preferred_element_type=F32).reshape(group, 2 * SLOTS, -1)[:, SLOTS:]
        both = (lo + hi).reshape(group * SLOTS, -1)
        unit = both.shape[1] // 2
        gate, up = both[:, :unit], both[:, unit:]
        act = (gate / (1.0 + jnp.exp(-gate)) * up).astype(BF16)
        step = 512
        for c in range(0, cols, step):
            y_lo = jnp.dot(act, wd[:, c : c + step], preferred_element_type=F32)
            y_hi = jnp.dot(act, wd[:, cols + c : cols + c + step], preferred_element_type=F32)
            y = jnp.concatenate(
                [y_lo.reshape(group, SLOTS, step), y_hi.reshape(group, SLOTS, step)], axis=1)
            y_buf[pl.ds(base, group), :, c : c + step] = y.astype(BF16)
        return carry

    if n == group:
        project(0, 0)
    else:
        lax.fori_loop(0, n // group, project, 0)

    def z_copy(slot, bit):
        return pltpu.make_async_remote_copy(
            src_ref=y_buf.at[slot], dst_ref=z_buf.at[slot], send_sem=z_send.at[slot], recv_sem=z_recv.at[slot],
            device_id=peer(bit), device_id_type=MESH)

    back = arrival[::-1]
    for slot in back + [0]:
        z_copy(slot ^ 1, 1).start()

    def summed(slot):
        value = y_buf[slot].astype(F32)
        for bit in [1] + later(slot)[::-1]:
            z_copy(slot ^ bit, bit).wait_recv()
            value += z_buf[slot ^ bit].astype(F32)
        return value

    for slot in back:
        y_buf[slot] = summed(slot).astype(BF16)
        z_copy(slot, last_bit(slot)).start()

    mine = summed(0)
    z_copy(half, half).wait_recv()
    theirs = z_buf[half].astype(F32)
    outs = []
    for part in range(2):
        sums = jnp.concatenate(
            [mine[part * SLOTS : (part + 1) * SLOTS], theirs[part * SLOTS : (part + 1) * SLOTS]], axis=0)
        span = slice(part * cols, (part + 1) * cols)
        mixed = jnp.dot(weighted, sums, preferred_element_type=F32, precision=lax.Precision.HIGHEST)
        out[:, span] = (hidden[:, span].astype(F32) + mixed).astype(BF16)
        outs.append(pltpu.make_async_copy(out.at[:, span], out_hbm.at[:, span], out_sem.at[part]))
        outs[-1].start()

    for copy in sent:
        copy.wait_send()
    for slot in range(1, n):
        z_copy(slot, last_bit(slot)).wait_send()
    for copy in outs:
        copy.wait()


def body(hidden, ln_gain, router, routes, w_gate, w_up, w_down):
    n = lax.axis_size("tok")
    tokens, width = hidden.shape
    units = w_gate.shape[-1]
    piece = (2 * SLOTS, width // 2)
    any_spec = pl.BlockSpec(memory_space=pl.ANY)
    vmem = pl.BlockSpec(memory_space=pltpu.VMEM)
    return pl.pallas_call(
        functools.partial(kernel, n),
        out_shape=jax.ShapeDtypeStruct((tokens, width), BF16),
        in_specs=[any_spec, vmem, any_spec, vmem, any_spec, any_spec, any_spec],
        out_specs=any_spec,
        scratch_shapes=[
            pltpu.VMEM((tokens, width), BF16),
            pltpu.VMEM(router.shape[::-1], BF16),
            pltpu.VMEM((width, units), BF16),
            pltpu.VMEM((width, units), BF16),
            pltpu.VMEM((units, width), BF16),
            pltpu.VMEM((n,) + piece, BF16),
            pltpu.VMEM(piece, BF16),
            pltpu.VMEM((n,) + piece, BF16),
            pltpu.VMEM((n,) + piece, BF16),
            pltpu.VMEM((tokens, width), BF16),
            pltpu.SemaphoreType.DMA((5,)),
            pltpu.SemaphoreType.DMA((2,)),
            pltpu.SemaphoreType.DMA((n,)),
            pltpu.SemaphoreType.DMA((n,)),
            pltpu.SemaphoreType.DMA((n,)),
            pltpu.SemaphoreType.DMA((n,)),
        ],
        compiler_params=pltpu.CompilerParams(
            collective_id=0, has_side_effects=True, vmem_limit_bytes=56 * 1024 * 1024
        ),
        name="expert_exchange",
    )(
        hidden,
        ln_gain.reshape(1, width),
        router.T,
        routes.T,
        w_gate.reshape(width, units),
        w_up.reshape(width, units),
        w_down.reshape(units, width),
    )


def solution(mesh):
    in_specs = (
        P(("group", "tok"), None),
        P(),
        P(),
        P(("group", "tok"), None),
        P("tok", None, None),
        P("tok", None, None),
        P("tok", None, None),
    )
    out_specs = P(("group", "tok"), None)
    return jax.shard_map(body, mesh=mesh, in_specs=in_specs, out_specs=out_specs, check_vma=False)
```

```python
import functools

import jax
import jax.numpy as jnp
from jax import lax
from jax.experimental import pallas as pl
from jax.experimental.pallas import tpu as pltpu
from jax.sharding import PartitionSpec as P

EXPERTS = 16
TOP = 4
EXP_WIN = 2
MB_ROWS = 64
MB_DEV = 2
MOST = 4
SLOTS = MB_DEV * MOST
TILE = 16
SPLIT = TILE // MOST

EPS = 1e-05
MESH = pl.DeviceIdType.MESH
F32 = jnp.float32
BF16 = jnp.bfloat16


def routes_plan(n):
    bits = n.bit_length() - 1
    inner = [1 << b for b in range(1, bits - 1)]
    half = n // 2
    orders = {0: inner[::-1], half: inner}

    def chain(slot):
        return half if slot & half else 0

    def later(slot):
        order = orders[chain(slot)]
        last = -1
        for at, bit in enumerate(order):
            if slot & bit:
                last = at
        return order[last + 1 :]

    def last_bit(slot):
        if slot & 1:
            return 1
        found = half
        for bit in orders[chain(slot)]:
            if slot & bit:
                found = bit
        return found

    evens = [slot for slot in range(n) if not slot & 1]

    def depth(slot):
        return bin(slot).count("1") + (1 if slot & half else 0)

    arrival = sorted([slot for slot in evens if slot], key=lambda slot: (depth(slot), slot & half))
    return later, last_bit, [(slot, depth(slot)) for slot in arrival]


def kernel(n, hidden_hbm, gain_ref, router_hbm, routes_ref, wg_hbm, wu_hbm, wd_hbm, out_hbm,
           hidden, router, wg, wu, wd, x_buf, other, y_buf, z_buf, out,
           in_sem, out_sem, x_send, x_recv, z_send, z_recv):
    later, last_bit, levels = routes_plan(n)
    arrival = [slot for slot, _ in levels]
    half = n // 2
    tokens, width = hidden.shape
    cols = width // SPLIT
    me = lax.axis_index("tok")

    def peer(bit):
        return {"tok": me + bit * (1 - 2 * lax.rem(lax.div(me, bit), 2))}

    load_hidden = pltpu.make_async_copy(hidden_hbm, hidden, in_sem.at[0])
    load_hidden.start()
    loads = [
        pltpu.make_async_copy(src, dst, in_sem.at[1 + at])
        for at, (src, dst) in enumerate(((router_hbm, router), (wg_hbm, wg), (wu_hbm, wu), (wd_hbm, wd)))
    ]
    for load in loads:
        load.start()

    barrier = pltpu.get_barrier_semaphore()
    bits = [1 << b for b in range(n.bit_length() - 1)]
    for bit in bits:
        pl.semaphore_signal(barrier, inc=1, device_id=peer(bit), device_id_type=MESH)

    my_expert = lax.div(me, half)
    token = lax.broadcasted_iota(jnp.int32, (2 * SLOTS, tokens), 1)
    slot_at = lax.broadcasted_iota(jnp.int32, (2 * SLOTS, tokens), 0)
    second = lax.rem(lax.div(slot_at, MOST), 2)
    slot_expert = my_expert + second - 2 * my_expert * second
    routes = routes_ref[...]
    hits = jnp.zeros((2 * SLOTS, tokens), F32)
    for k in range(TOP):
        hits += jnp.where(routes[k : k + 1] == slot_expert, 1.0, 0.0)
    row = lax.broadcasted_iota(jnp.int32, (tokens, tokens), 0)
    lane = lax.broadcasted_iota(jnp.int32, (tokens, tokens), 1)
    earlier = (row < lane) & (lax.div(lane, MB_ROWS) == lax.div(row, MB_ROWS))
    rank = jnp.dot(hits.astype(BF16), jnp.where(earlier, 1.0, 0.0).astype(BF16), preferred_element_type=F32)
    slot_rank = lax.rem(slot_at, MOST)
    slot_block = lax.div(slot_at, SLOTS)
    fits = (rank == slot_rank.astype(F32)) & (slot_block == lax.div(token, MB_ROWS))
    pick = jnp.where(fits, hits, 0.0)

    load_hidden.wait()
    rows = jnp.dot(pick.astype(BF16), hidden[...], preferred_element_type=F32)
    center = jnp.mean(rows, axis=-1, keepdims=True)
    rows = rows - center
    spread = jnp.mean(jnp.square(rows), axis=-1, keepdims=True)
    rows = rows * lax.rsqrt(spread + EPS) * gain_ref[...].astype(F32).reshape(1, width)

    normed = rows.astype(BF16)

    pieces = MB_DEV * EXP_WIN
    spread_row = lax.broadcasted_iota(jnp.int32, (pieces * TILE, SPLIT * TILE), 0)
    spread_col = lax.broadcasted_iota(jnp.int32, (pieces * TILE, SPLIT * TILE), 1)
    same_slot = (lax.div(spread_row, TILE) == lax.div(lax.rem(spread_col, TILE), MOST)) & (
        lax.rem(spread_row, MOST) == lax.rem(spread_col, MOST))
    same_part = lax.div(lax.rem(spread_row, TILE), MOST) == lax.div(spread_col, TILE)
    spread_out = jnp.where(same_slot & same_part, 1.0, 0.0).astype(BF16)
    stacked = jnp.concatenate([normed[:, part * cols : (part + 1) * cols] for part in range(SPLIT)], axis=0)
    cut = jnp.dot(spread_out, stacked, preferred_element_type=F32).astype(BF16)
    for mb in range(MB_DEV):
        at = mb * 2 * TILE
        x_buf[mb, 0] = cut[at : at + TILE]
        other[mb] = cut[at + TILE : at + 2 * TILE]

    pl.semaphore_wait(barrier, len(bits))

    def x_copy(mb, src, slot, bit):
        return pltpu.make_async_remote_copy(
            src_ref=src, dst_ref=x_buf.at[mb, slot], send_sem=x_send.at[mb, slot], recv_sem=x_recv.at[mb, slot],
            device_id=peer(bit), device_id_type=MESH)

    sent = []

    def pass_on(mb, slot):
        for bit in later(slot) + [1]:
            sent.append(x_copy(mb, x_buf.at[mb, slot], slot ^ bit, bit))
            sent[-1].start()

    for mb in range(MB_DEV):
        sent.append(x_copy(mb, other.at[mb], half, half))
        sent[-1].start()
        pass_on(mb, 0)

    loads[0].wait()
    across = (((1,), (1,)), ((), ()))
    logits = lax.dot_general(normed, router[...], across, preferred_element_type=F32)
    expert_row = lax.broadcasted_iota(jnp.int32, (EXPERTS, tokens), 0)
    chosen = jnp.zeros((EXPERTS, tokens), F32)
    for k in range(TOP):
        chosen += jnp.where(routes[k : k + 1] == expert_row, 1.0, 0.0)
    slot_chosen = lax.dot_general(pick.astype(BF16), chosen.astype(BF16), across, preferred_element_type=F32)
    raised = jnp.where(slot_chosen > 0.5, jnp.exp(logits), 0.0)
    expert_lane = lax.broadcasted_iota(jnp.int32, (2 * SLOTS, EXPERTS), 1)
    top = jnp.sum(jnp.where(expert_lane == slot_expert[:, :EXPERTS], raised, 0.0), axis=-1, keepdims=True)
    total = jnp.sum(raised, axis=-1, keepdims=True)
    filled = jnp.sum(slot_chosen, axis=-1, keepdims=True) > 0.5
    gates = jnp.where(filled, top / jnp.where(filled, total, 1.0), 0.0)
    weighted = pick * gates
    weights = []
    lane_part = lax.rem(lax.div(lax.broadcasted_iota(jnp.int32, (MB_ROWS, 128), 1), MOST), SPLIT)
    high = weighted.astype(BF16).astype(F32)
    low = weighted - high
    for mb in range(MB_DEV):
        def four(values, e):
            at = mb * SLOTS + e * MOST
            return [values[at : at + MOST]] * SPLIT
        tall = four(high, 0) + four(high, 1) + four(low, 0) + four(low, 1) + four(high, 0)
        tall = jnp.concatenate(tall + [jnp.zeros((128 - 5 * TILE, tokens), F32)], axis=0).T
        tall = tall[mb * MB_ROWS : (mb + 1) * MB_ROWS]
        weights.append([jnp.where(lane_part == part, tall, 0.0).astype(BF16) for part in range(SPLIT)])

    def arrive(mb, slot):
        x_copy(mb, other.at[mb], slot, last_bit(slot)).wait_recv()
        if not slot & 1:
            pass_on(mb, slot)

    group = min(n, 16)
    tall_rows = group * TILE
    part_of = lax.rem(lax.div(lax.broadcasted_iota(jnp.int32, (tall_rows, 1), 0), MOST), SPLIT)
    one = lax.broadcasted_iota(jnp.int32, (tall_rows, tall_rows), 0)
    two = lax.broadcasted_iota(jnp.int32, (tall_rows, tall_rows), 1)
    same = (lax.div(one, TILE) == lax.div(two, TILE)) & (lax.rem(one, MOST) == lax.rem(two, MOST))
    gather_parts = jnp.where(same, 1.0, 0.0)

    def project(mb):
        def step_of(at, carry):
            base = pl.multiple_of(at * group, group)
            x = x_buf[mb, pl.ds(base, group)].reshape(tall_rows, cols)
            both = jnp.zeros((tall_rows, 2 * wg.shape[1]), F32)
            for part in range(SPLIT):
                span = slice(part * cols, (part + 1) * cols)
                w = jnp.concatenate([wg[span], wu[span]], axis=1)
                both += jnp.where(part_of == part, jnp.dot(x, w, preferred_element_type=F32), 0.0)
            both = jnp.dot(gather_parts, both, preferred_element_type=F32, precision=lax.Precision.HIGHEST)
            unit = both.shape[1] // 2
            gate, up = both[:, :unit], both[:, unit:]
            act = gate / (1.0 + jnp.exp(-gate)) * up
            act = jnp.concatenate(
                [jnp.where(part_of == part, act, 0.0).astype(BF16) for part in range(SPLIT)], axis=1)
            step = 512
            for c in range(0, cols, step):
                w = jnp.concatenate(
                    [wd[:, part * cols + c : part * cols + c + step] for part in range(SPLIT)], axis=0)
                y = jnp.dot(act, w, preferred_element_type=F32)
                y_buf[mb, pl.ds(base, group), :, c : c + step] = y.reshape(group, TILE, step).astype(BF16)
            return carry

        if n == group:
            step_of(0, 0)
        else:
            lax.fori_loop(0, n // group, step_of, 0)

    def z_copy(mb, slot, bit):
        return pltpu.make_async_remote_copy(
            src_ref=y_buf.at[mb, slot], dst_ref=z_buf.at[mb, slot],
            send_sem=z_send.at[mb, slot], recv_sem=z_recv.at[mb, slot],
            device_id=peer(bit), device_id_type=MESH)

    back = levels[::-1]

    def start_back(mb):
        for slot in arrival[::-1] + [0]:
            z_copy(mb, slot ^ 1, 1).start()

    def summed(mb, slot):
        value = y_buf[mb, slot].astype(F32)
        for bit in [1] + later(slot)[::-1]:
            z_copy(mb, slot ^ bit, bit).wait_recv()
            value += z_buf[mb, slot ^ bit].astype(F32)
        return value

    def send_back(mb, slot):
        y_buf[mb, slot] = summed(mb, slot).astype(BF16)
        z_copy(mb, slot, last_bit(slot)).start()

    outs = []

    def finish(mb):
        mine = summed(mb, 0)
        z_copy(mb, half, half).wait_recv()
        theirs = z_buf[mb, half]
        mine_high = mine.astype(BF16)
        mine_low = (mine - mine_high.astype(F32)).astype(BF16)
        sums = jnp.concatenate(
            [mine_high, theirs, mine_high, theirs, mine_low, jnp.zeros((128 - 5 * TILE, cols), BF16)], axis=0)
        span = slice(mb * MB_ROWS, (mb + 1) * MB_ROWS)
        mixed = jnp.dot(jnp.concatenate(weights[mb], axis=0), sums, preferred_element_type=F32)
        for part in range(SPLIT):
            at = slice(part * cols, (part + 1) * cols)
            term = mixed[part * MB_ROWS : (part + 1) * MB_ROWS]
            out[span, at] = (hidden[span, at].astype(F32) + term).astype(BF16)
        outs.append(pltpu.make_async_copy(out.at[span], out_hbm.at[span], out_sem.at[mb]))
        outs[-1].start()

    deepest = max(level for _, level in levels)
    for level in range(1, deepest + 2):
        for mb in range(MB_DEV):
            for slot, at in levels:
                if at == level - mb:
                    arrive(mb, slot)
        if level == deepest:
            for slot in range(1, n, 2):
                arrive(0, slot)
            for load in loads[1:]:
                load.wait()
            project(0)
            start_back(0)
    first = [slot for slot, at in back if at == deepest]
    for slot in first:
        send_back(0, slot)
    for slot in range(1, n, 2):
        arrive(1, slot)
    project(1)
    start_back(1)
    for level in range(deepest - 1, -1, -1):
        for mb in range(MB_DEV):
            for slot, at in back:
                if at == level + mb:
                    send_back(mb, slot)
        if level == 0:
            for mb in range(MB_DEV):
                finish(mb)

    for copy in sent:
        copy.wait_send()
    for mb in range(MB_DEV):
        for slot in range(1, n):
            z_copy(mb, slot, last_bit(slot)).wait_send()
    for copy in outs:
        copy.wait()


def body(hidden, ln_gain, router, routes, w_gate, w_up, w_down):
    n = lax.axis_size("tok")
    tokens, width = hidden.shape
    units = w_gate.shape[-1]
    piece = (TILE, width // SPLIT)
    any_spec = pl.BlockSpec(memory_space=pl.ANY)
    vmem = pl.BlockSpec(memory_space=pltpu.VMEM)
    return pl.pallas_call(
        functools.partial(kernel, n),
        out_shape=jax.ShapeDtypeStruct((tokens, width), BF16),
        in_specs=[any_spec, vmem, any_spec, vmem, any_spec, any_spec, any_spec],
        out_specs=any_spec,
        scratch_shapes=[
            pltpu.VMEM((tokens, width), BF16),
            pltpu.VMEM(router.shape[::-1], BF16),
            pltpu.VMEM((width, units), BF16),
            pltpu.VMEM((width, units), BF16),
            pltpu.VMEM((units, width), BF16),
            pltpu.VMEM((MB_DEV, n) + piece, BF16),
            pltpu.VMEM((MB_DEV,) + piece, BF16),
            pltpu.VMEM((MB_DEV, n) + piece, BF16),
            pltpu.VMEM((MB_DEV, n) + piece, BF16),
            pltpu.VMEM((tokens, width), BF16),
            pltpu.SemaphoreType.DMA((5,)),
            pltpu.SemaphoreType.DMA((2,)),
            pltpu.SemaphoreType.DMA((MB_DEV, n)),
            pltpu.SemaphoreType.DMA((MB_DEV, n)),
            pltpu.SemaphoreType.DMA((MB_DEV, n)),
            pltpu.SemaphoreType.DMA((MB_DEV, n)),
        ],
        compiler_params=pltpu.CompilerParams(
            collective_id=0, has_side_effects=True, vmem_limit_bytes=56 * 1024 * 1024
        ),
        name="expert_exchange",
    )(
        hidden,
        ln_gain,
        router.T,
        routes.T,
        w_gate.reshape(width, units),
        w_up.reshape(width, units),
        w_down.reshape(units, width),
    )


def solution(mesh):
    in_specs = (
        P(("group", "tok"), None),
        P(),
        P(),
        P(("group", "tok"), None),
        P("tok", None, None),
        P("tok", None, None),
        P("tok", None, None),
    )
    out_specs = P(("group", "tok"), None)
    return jax.shard_map(body, mesh=mesh, in_specs=in_specs, out_specs=out_specs, check_vma=False)
```

```python
import functools

import jax
import jax.numpy as jnp
from jax import lax
from jax.experimental import pallas as pl
from jax.experimental.pallas import tpu as pltpu
from jax.sharding import PartitionSpec as P

EXPERTS = 16
TOP = 4
EXP_WIN = 2
MB_ROWS = 64
MB_DEV = 2
MOST = 4
SLOTS = MB_DEV * MOST
TILE = 16
SPLIT = TILE // MOST

EPS = 1e-05
MESH = pl.DeviceIdType.MESH
F32 = jnp.float32
BF16 = jnp.bfloat16


def routes_plan(n):
    bits = n.bit_length() - 1
    inner = [1 << b for b in range(1, bits - 1)]
    half = n // 2
    orders = {0: inner[::-1], half: inner}

    def chain(slot):
        return half if slot & half else 0

    def later(slot):
        order = orders[chain(slot)]
        last = -1
        for at, bit in enumerate(order):
            if slot & bit:
                last = at
        return order[last + 1 :]

    def last_bit(slot):
        if slot & 1:
            return 1
        found = half
        for bit in orders[chain(slot)]:
            if slot & bit:
                found = bit
        return found

    evens = [slot for slot in range(n) if not slot & 1]

    def depth(slot):
        return bin(slot).count("1") + (1 if slot & half else 0)

    arrival = sorted([slot for slot in evens if slot], key=lambda slot: (depth(slot), slot & half))
    return later, last_bit, [(slot, depth(slot)) for slot in arrival]


def kernel(n, hidden_hbm, gain_ref, router_hbm, routes_ref, wg_hbm, wu_hbm, wd_hbm, out_hbm,
           hidden, router, wg, wu, wd, x_buf, other, y_buf, z_buf, out,
           in_sem, out_sem, x_send, x_recv, z_send, z_recv):
    later, last_bit, levels = routes_plan(n)
    arrival = [slot for slot, _ in levels]
    half = n // 2
    tokens, width = hidden.shape
    cols = width // SPLIT
    me = lax.axis_index("tok")

    def peer(bit):
        return {"tok": me + bit * (1 - 2 * lax.rem(lax.div(me, bit), 2))}

    load_hidden = pltpu.make_async_copy(hidden_hbm, hidden, in_sem.at[0])
    load_hidden.start()
    loads = [
        pltpu.make_async_copy(src, dst, in_sem.at[1 + at])
        for at, (src, dst) in enumerate(((router_hbm, router), (wg_hbm, wg), (wu_hbm, wu), (wd_hbm, wd)))
    ]
    for load in loads:
        load.start()

    barrier = pltpu.get_barrier_semaphore()
    bits = [1 << b for b in range(n.bit_length() - 1)]
    for bit in bits:
        pl.semaphore_signal(barrier, inc=1, device_id=peer(bit), device_id_type=MESH)

    my_expert = lax.div(me, half)
    token = lax.broadcasted_iota(jnp.int32, (2 * SLOTS, tokens), 1)
    slot_at = lax.broadcasted_iota(jnp.int32, (2 * SLOTS, tokens), 0)
    second = lax.rem(lax.div(slot_at, MOST), 2)
    slot_expert = my_expert + second - 2 * my_expert * second
    routes = routes_ref[...]
    hits = jnp.zeros((2 * SLOTS, tokens), F32)
    for k in range(TOP):
        hits += jnp.where(routes[k : k + 1] == slot_expert, 1.0, 0.0)
    row = lax.broadcasted_iota(jnp.int32, (tokens, tokens), 0)
    lane = lax.broadcasted_iota(jnp.int32, (tokens, tokens), 1)
    earlier = (row < lane) & (lax.div(lane, MB_ROWS) == lax.div(row, MB_ROWS))
    rank = jnp.dot(hits.astype(BF16), jnp.where(earlier, 1.0, 0.0).astype(BF16), preferred_element_type=F32)
    slot_rank = lax.rem(slot_at, MOST)
    slot_block = lax.div(slot_at, SLOTS)
    fits = (rank == slot_rank.astype(F32)) & (slot_block == lax.div(token, MB_ROWS))
    pick = jnp.where(fits, hits, 0.0)

    load_hidden.wait()
    rows = jnp.dot(pick.astype(BF16), hidden[...], preferred_element_type=F32)
    center = jnp.mean(rows, axis=-1, keepdims=True)
    rows = rows - center
    spread = jnp.mean(jnp.square(rows), axis=-1, keepdims=True)
    rows = rows * lax.rsqrt(spread + EPS) * gain_ref[...].astype(F32).reshape(1, width)

    normed = rows.astype(BF16)

    pieces = MB_DEV * EXP_WIN
    spread_row = lax.broadcasted_iota(jnp.int32, (pieces * TILE, SPLIT * TILE), 0)
    spread_col = lax.broadcasted_iota(jnp.int32, (pieces * TILE, SPLIT * TILE), 1)
    same_slot = (lax.div(spread_row, TILE) == lax.div(lax.rem(spread_col, TILE), MOST)) & (
        lax.rem(spread_row, MOST) == lax.rem(spread_col, MOST))
    same_part = lax.div(lax.rem(spread_row, TILE), MOST) == lax.div(spread_col, TILE)
    spread_out = jnp.where(same_slot & same_part, 1.0, 0.0).astype(BF16)
    stacked = jnp.concatenate([normed[:, part * cols : (part + 1) * cols] for part in range(SPLIT)], axis=0)
    cut = jnp.dot(spread_out, stacked, preferred_element_type=F32).astype(BF16)
    for mb in range(MB_DEV):
        at = mb * 2 * TILE
        x_buf[mb, 0] = cut[at : at + TILE]
        other[mb] = cut[at + TILE : at + 2 * TILE]

    pl.semaphore_wait(barrier, len(bits))

    def x_copy(mb, src, slot, bit):
        return pltpu.make_async_remote_copy(
            src_ref=src, dst_ref=x_buf.at[mb, slot], send_sem=x_send.at[mb, slot], recv_sem=x_recv.at[mb, slot],
            device_id=peer(bit), device_id_type=MESH)

    sent = []

    def pass_on(mb, slot):
        for bit in later(slot) + [1]:
            sent.append(x_copy(mb, x_buf.at[mb, slot], slot ^ bit, bit))
            sent[-1].start()

    for mb in range(MB_DEV):
        sent.append(x_copy(mb, other.at[mb], half, half))
        sent[-1].start()
    for mb in range(MB_DEV):
        pass_on(mb, 0)

    loads[0].wait()
    across = (((1,), (1,)), ((), ()))
    logits = lax.dot_general(normed, router[...], across, preferred_element_type=F32)
    expert_row = lax.broadcasted_iota(jnp.int32, (EXPERTS, tokens), 0)
    chosen = jnp.zeros((EXPERTS, tokens), F32)
    for k in range(TOP):
        chosen += jnp.where(routes[k : k + 1] == expert_row, 1.0, 0.0)
    slot_chosen = lax.dot_general(pick.astype(BF16), chosen.astype(BF16), across, preferred_element_type=F32)
    raised = jnp.where(slot_chosen > 0.5, jnp.exp(logits), 0.0)
    expert_lane = lax.broadcasted_iota(jnp.int32, (2 * SLOTS, EXPERTS), 1)
    top = jnp.sum(jnp.where(expert_lane == slot_expert[:, :EXPERTS], raised, 0.0), axis=-1, keepdims=True)
    total = jnp.sum(raised, axis=-1, keepdims=True)
    filled = jnp.sum(slot_chosen, axis=-1, keepdims=True) > 0.5
    gates = jnp.where(filled, top / jnp.where(filled, total, 1.0), 0.0)
    weighted = pick * gates
    weights = []
    lane_part = lax.rem(lax.div(lax.broadcasted_iota(jnp.int32, (MB_ROWS, 128), 1), MOST), SPLIT)
    high = weighted.astype(BF16).astype(F32)
    low = weighted - high
    for mb in range(MB_DEV):
        def four(values, e):
            at = mb * SLOTS + e * MOST
            return [values[at : at + MOST]] * SPLIT
        tall = four(high, 0) + four(high, 1) + four(low, 0) + four(low, 1) + four(high, 0)
        tall = jnp.concatenate(tall + [jnp.zeros((128 - 5 * TILE, tokens), F32)], axis=0).T
        tall = tall[mb * MB_ROWS : (mb + 1) * MB_ROWS]
        weights.append([jnp.where(lane_part == part, tall, 0.0).astype(BF16) for part in range(SPLIT)])

    def arrive(mb, slot):
        x_copy(mb, other.at[mb], slot, last_bit(slot)).wait_recv()
        if not slot & 1:
            pass_on(mb, slot)

    group = min(n, 16)
    tall_rows = group * TILE
    part_of = lax.rem(lax.div(lax.broadcasted_iota(jnp.int32, (tall_rows, 1), 0), MOST), SPLIT)
    one = lax.broadcasted_iota(jnp.int32, (tall_rows, tall_rows), 0)
    two = lax.broadcasted_iota(jnp.int32, (tall_rows, tall_rows), 1)
    same = (lax.div(one, TILE) == lax.div(two, TILE)) & (lax.rem(one, MOST) == lax.rem(two, MOST))
    gather_parts = jnp.where(same, 1.0, 0.0)

    def project(mb):
        def step_of(at, carry):
            base = pl.multiple_of(at * group, group)
            x = x_buf[mb, pl.ds(base, group)].reshape(tall_rows, cols)
            both = jnp.zeros((tall_rows, 2 * wg.shape[1]), F32)
            for part in range(SPLIT):
                span = slice(part * cols, (part + 1) * cols)
                w = jnp.concatenate([wg[span], wu[span]], axis=1)
                both += jnp.where(part_of == part, jnp.dot(x, w, preferred_element_type=F32), 0.0)
            both = jnp.dot(gather_parts, both, preferred_element_type=F32, precision=lax.Precision.HIGHEST)
            unit = both.shape[1] // 2
            gate, up = both[:, :unit], both[:, unit:]
            act = gate / (1.0 + jnp.exp(-gate)) * up
            act = jnp.concatenate(
                [jnp.where(part_of == part, act, 0.0).astype(BF16) for part in range(SPLIT)], axis=1)
            step = 512
            for c in range(0, cols, step):
                w = jnp.concatenate(
                    [wd[:, part * cols + c : part * cols + c + step] for part in range(SPLIT)], axis=0)
                y = jnp.dot(act, w, preferred_element_type=F32)
                y_buf[mb, pl.ds(base, group), :, c : c + step] = y.reshape(group, TILE, step).astype(BF16)
            return carry

        if n == group:
            step_of(0, 0)
        else:
            lax.fori_loop(0, n // group, step_of, 0)

    def z_copy(mb, slot, bit):
        return pltpu.make_async_remote_copy(
            src_ref=y_buf.at[mb, slot], dst_ref=z_buf.at[mb, slot],
            send_sem=z_send.at[mb, slot], recv_sem=z_recv.at[mb, slot],
            device_id=peer(bit), device_id_type=MESH)

    back = levels[::-1]

    def start_back(mb):
        for slot in arrival[::-1] + [0]:
            z_copy(mb, slot ^ 1, 1).start()

    def summed(mb, slot):
        value = y_buf[mb, slot].astype(F32)
        for bit in [1] + later(slot)[::-1]:
            z_copy(mb, slot ^ bit, bit).wait_recv()
            value += z_buf[mb, slot ^ bit].astype(F32)
        return value

    def send_back(mb, slot):
        y_buf[mb, slot] = summed(mb, slot).astype(BF16)
        z_copy(mb, slot, last_bit(slot)).start()

    outs = []

    def finish(mb):
        mine = summed(mb, 0)
        z_copy(mb, half, half).wait_recv()
        theirs = z_buf[mb, half]
        mine_high = mine.astype(BF16)
        mine_low = (mine - mine_high.astype(F32)).astype(BF16)
        sums = jnp.concatenate(
            [mine_high, theirs, mine_high, theirs, mine_low, jnp.zeros((128 - 5 * TILE, cols), BF16)], axis=0)
        span = slice(mb * MB_ROWS, (mb + 1) * MB_ROWS)
        mixed = jnp.dot(jnp.concatenate(weights[mb], axis=0), sums, preferred_element_type=F32)
        for part in range(SPLIT):
            at = slice(part * cols, (part + 1) * cols)
            term = mixed[part * MB_ROWS : (part + 1) * MB_ROWS]
            out[span, at] = (hidden[span, at].astype(F32) + term).astype(BF16)
        outs.append(pltpu.make_async_copy(out.at[span], out_hbm.at[span], out_sem.at[mb]))
        outs[-1].start()

    deepest = max(level for _, level in levels)
    for level in range(1, deepest + 2):
        for mb in range(MB_DEV):
            for slot, at in levels:
                if at == level - mb:
                    arrive(mb, slot)
        if level == deepest:
            for slot in range(1, n, 2):
                arrive(0, slot)
            for load in loads[1:]:
                load.wait()
            project(0)
            start_back(0)
    first = [slot for slot, at in back if at == deepest]
    for slot in first:
        send_back(0, slot)
    for slot in range(1, n, 2):
        arrive(1, slot)
    project(1)
    start_back(1)
    for slot in first:
        send_back(1, slot)
    for level in range(deepest - 1, -1, -1):
        for mb in range(MB_DEV):
            for slot, at in back:
                if at == level:
                    send_back(mb, slot)
        if level == 0:
            for mb in range(MB_DEV):
                finish(mb)

    for copy in sent:
        copy.wait_send()
    for mb in range(MB_DEV):
        for slot in range(1, n):
            z_copy(mb, slot, last_bit(slot)).wait_send()
    for copy in outs:
        copy.wait()


def body(hidden, ln_gain, router, routes, w_gate, w_up, w_down):
    n = lax.axis_size("tok")
    tokens, width = hidden.shape
    units = w_gate.shape[-1]
    piece = (TILE, width // SPLIT)
    any_spec = pl.BlockSpec(memory_space=pl.ANY)
    vmem = pl.BlockSpec(memory_space=pltpu.VMEM)
    return pl.pallas_call(
        functools.partial(kernel, n),
        out_shape=jax.ShapeDtypeStruct((tokens, width), BF16),
        in_specs=[any_spec, vmem, any_spec, vmem, any_spec, any_spec, any_spec],
        out_specs=any_spec,
        scratch_shapes=[
            pltpu.VMEM((tokens, width), BF16),
            pltpu.VMEM(router.shape[::-1], BF16),
            pltpu.VMEM((width, units), BF16),
            pltpu.VMEM((width, units), BF16),
            pltpu.VMEM((units, width), BF16),
            pltpu.VMEM((MB_DEV, n) + piece, BF16),
            pltpu.VMEM((MB_DEV,) + piece, BF16),
            pltpu.VMEM((MB_DEV, n) + piece, BF16),
            pltpu.VMEM((MB_DEV, n) + piece, BF16),
            pltpu.VMEM((tokens, width), BF16),
            pltpu.SemaphoreType.DMA((5,)),
            pltpu.SemaphoreType.DMA((2,)),
            pltpu.SemaphoreType.DMA((MB_DEV, n)),
            pltpu.SemaphoreType.DMA((MB_DEV, n)),
            pltpu.SemaphoreType.DMA((MB_DEV, n)),
            pltpu.SemaphoreType.DMA((MB_DEV, n)),
        ],
        compiler_params=pltpu.CompilerParams(
            collective_id=0, has_side_effects=True, vmem_limit_bytes=56 * 1024 * 1024
        ),
        name="expert_exchange",
    )(
        hidden,
        ln_gain,
        router.T,
        routes.T,
        w_gate.reshape(width, units),
        w_up.reshape(width, units),
        w_down.reshape(units, width),
    )


def solution(mesh):
    in_specs = (
        P(("group", "tok"), None),
        P(),
        P(),
        P(("group", "tok"), None),
        P("tok", None, None),
        P("tok", None, None),
        P("tok", None, None),
    )
    out_specs = P(("group", "tok"), None)
    return jax.shard_map(body, mesh=mesh, in_specs=in_specs, out_specs=out_specs, check_vma=False)
```
